512 devices in a mesh: ctx: 64 (over y, z_hi, x), head: 8 (over z_lo, core).
Axes of the slice: x: 4, y: 8, z: 8 (z_hi: 2, z_lo: 4; z = z_hi * 4 + z_lo), core: 2. Of those that a mesh axis runs over, the one named last changes fastest.
Arguments:
- queries: bfloat16 [16384, 16384], P('ctx', 'head'), may hold values from -6 to 6
- keys: bfloat16 [16384, 1024], P(('ctx', 'head')), may hold values from -6 to 6
- values: bfloat16 [16384, 1024], P(('ctx', 'head')), may hold values from -0.5390625 to 0.5390625
- out_grad: bfloat16 [16384, 16384], P('ctx', 'head'), may hold values from -96 to 96
- log_norm: float32 [128, 16384], P('head', 'ctx'), as said below
- delta_rows: float32 [128, 16384], P('head', 'ctx'), may hold values from -96 to 96
- doc_start: int32 [16384], P('ctx'), may hold values from 0 to 16383, as said below
Outputs:
- query_grad: bfloat16 [16384, 16384], P('ctx', 'head')
- key_grad: bfloat16 [16384, 1024], P(('ctx', 'head'))
- value_grad: bfloat16 [16384, 1024], P(('ctx', 'head'))
The draws below stay inside these ranges and needn't reach their ends.
Inputs may be any that keep to these rules, and one draw needn't show every extreme that they name: Documents are contiguous runs of positions; doc_start[p] is the first position of p's document. Each document has 1 to 1024 tokens; one has exactly 1024 tokens and does not begin at a multiple of 256; the last position is a document of its own. log_norm[i, p] lies within 0.5 of 0.5 plus the natural logarithm of p - doc_start[p] + 1.
All inputs are finite; a program needn't handle non-finite values.
Results may differ from the reference program's by a relative error of at most 0.0052.
Values may be sent and summed in bfloat16 or wider, within the bound.
No kernel may reach another device: no remote copies, remote signals or barrier semaphores. Data moves between devices by JAX's collectives and lax.ppermute only.
A program may use at most 64 MiB of HBM per device.

```python
import jax
import jax.numpy as jnp
from jax import lax

HEADS = 128
KVG = 8
HD = 128
TOK_DEV = 256
REACH = 4
GROUP_HEADS = 16
DOC_MOST = 1024
TOKENS = 16384
N_CTX = 64


def doc_layout(key):
    first_key, second_key, third_key, fourth_key = jax.random.split(key, 4)
    short_len = jax.random.randint(first_key, (TOKENS,), 1, DOC_MOST + 1)
    full_len = DOC_MOST - jax.random.randint(second_key, (TOKENS,), 0, TOK_DEV)
    coin = jax.random.randint(third_key, (TOKENS,), 0, 2)
    lengths = jnp.where(coin == 1, full_len, short_len).astype(jnp.int32)
    lengths = lengths.at[0].set(jax.random.randint(fourth_key, (), 1, TOK_DEV).astype(jnp.int32))
    lengths = lengths.at[1].set(DOC_MOST)
    ends = jnp.cumsum(lengths).astype(jnp.int32)
    starts = (ends - lengths).astype(jnp.int32)
    positions = jnp.arange(TOKENS, dtype=jnp.int32)
    which = jnp.searchsorted(ends, positions, side='right').astype(jnp.int32)
    result = starts[which]
    return result.at[TOKENS - 1].set(TOKENS - 1).astype(jnp.int32)


def draw_doc_start(key, part):
    return doc_layout(key)


def draw_log_norm(key, part):
    starts = doc_layout(key)
    key = jax.random.fold_in(key, 7)
    positions = jnp.arange(TOKENS, dtype=jnp.int32)
    visible = (positions - starts + 1).astype(jnp.float32)
    offset = jax.random.uniform(key, (HEADS, TOKENS), jnp.float32, -0.5, 0.5)
    return (jnp.log(visible)[None, :] + 0.5 + offset).astype(jnp.float32)


def level_of(rng, dims, shards, least, top_value):
    gain, own = 1.0, jax.random.fold_in(rng, 6)
    for position, parts in shards:
        heights = jnp.exp(jax.random.uniform(jax.random.fold_in(own, position), (parts,), jnp.float32, least / len(shards), top_value / len(shards)))
        gain = gain * jnp.repeat(heights, dims[position] // parts).reshape([-1 if axis == position else 1 for axis in range(len(dims))])
    return gain


def normal_values(rng, extent, spread, limit, cuts=(), kind=jnp.bfloat16):
    values = spread * jax.random.normal(rng, extent, jnp.float32)
    if cuts:
        values = values * level_of(rng, extent, cuts, -0.22, 0.18)
    return jnp.clip(values, -limit, limit).astype(kind)


def setup_inputs(seed: int = 0) -> dict:
    key_list = jax.random.split(jax.random.key(seed), 8)
    return {
        "queries": normal_values(key_list[0], (TOKENS, HEADS * HD), 1.0, 6.0, ((0, 64), (1, 8))),
        "keys": normal_values(key_list[1], (TOKENS, KVG * HD), 1.0, 6.0, ((0, 512),)),
        "values": normal_values(key_list[2], (TOKENS, KVG * HD), 0.09, 0.5390625, ((0, 512),)),
        "out_grad": normal_values(key_list[3], (TOKENS, HEADS * HD), 16.0, 96.0, ((0, 64), (1, 8))),
        "log_norm": draw_log_norm(jax.random.fold_in(key_list[7], 71), 0),
        "delta_rows": normal_values(key_list[5], (HEADS, TOKENS), 16.0, 96.0, ((0, 8), (1, 64)), jnp.float32),
        "doc_start": draw_doc_start(jax.random.fold_in(key_list[7], 71), 0),
    }


def rounded(array):
    return lax.optimization_barrier(array.astype(jnp.bfloat16)).astype(jnp.float32)


def reference(queries, keys, values, out_grad, log_norm, delta_rows, doc_start):
    scale = HD ** -0.5
    rows = TOK_DEV
    margin = REACH * rows
    span = margin + rows
    query_all = queries.astype(jnp.float32).reshape(TOKENS, KVG, GROUP_HEADS, HD)
    grad_all = out_grad.astype(jnp.float32).reshape(TOKENS, KVG, GROUP_HEADS, HD)
    norm_all = log_norm.reshape(KVG, GROUP_HEADS, TOKENS)
    delta_all = delta_rows.reshape(KVG, GROUP_HEADS, TOKENS)
    front = jnp.zeros((margin, KVG, HD), jnp.float32)
    key_padded = jnp.concatenate([front, keys.astype(jnp.float32).reshape(TOKENS, KVG, HD)], 0)
    value_padded = jnp.concatenate([front, values.astype(jnp.float32).reshape(TOKENS, KVG, HD)], 0)

    def step(carry, block):
        key_acc, value_acc = carry
        start = (block * rows).astype(jnp.int32)
        query_block = lax.dynamic_slice_in_dim(query_all, start, rows, 0)
        grad_block = lax.dynamic_slice_in_dim(grad_all, start, rows, 0)
        norm_block = lax.dynamic_slice_in_dim(norm_all, start, rows, 2)
        delta_block = lax.dynamic_slice_in_dim(delta_all, start, rows, 2)
        first = lax.dynamic_slice_in_dim(doc_start, start, rows, 0)
        key_window = lax.dynamic_slice_in_dim(key_padded, start, span, 0)
        value_window = lax.dynamic_slice_in_dim(value_padded, start, span, 0)
        query_pos = start + jnp.arange(rows, dtype=jnp.int32)
        key_pos = start - margin + jnp.arange(span, dtype=jnp.int32)
        allowed = (key_pos[None, :] >= first[:, None]) & (key_pos[None, :] <= query_pos[:, None])
        scores = jnp.einsum('qghd,kgd->ghqk', query_block, key_window) * scale
        probs = jnp.where(allowed[None, None], jnp.exp(scores - norm_block[..., None]), 0.0)
        probs_b = rounded(probs)
        value_term = jnp.einsum('ghqk,qghd->kgd', probs_b, grad_block)
        dprobs = jnp.einsum('qghd,kgd->ghqk', grad_block, value_window)
        dscores = rounded(probs * (dprobs - delta_block[..., None]))
        query_term = jnp.einsum('ghqk,kgd->qghd', dscores, key_window) * scale
        key_term = jnp.einsum('ghqk,qghd->kgd', dscores, query_block) * scale
        key_acc = lax.dynamic_update_slice_in_dim(key_acc, lax.dynamic_slice_in_dim(key_acc, start, span, 0) + key_term, start, 0)
        value_acc = lax.dynamic_update_slice_in_dim(value_acc, lax.dynamic_slice_in_dim(value_acc, start, span, 0) + value_term, start, 0)
        return (key_acc, value_acc), query_term.astype(jnp.bfloat16)

    empty = jnp.zeros((TOKENS + margin, KVG, HD), jnp.float32)
    (key_acc, value_acc), query_blocks = lax.scan(step, (empty, empty), jnp.arange(N_CTX, dtype=jnp.int32))
    query_grad = query_blocks.reshape(TOKENS, HEADS * HD)
    key_grad = key_acc[margin:].reshape(TOKENS, KVG * HD).astype(jnp.bfloat16)
    value_grad = value_acc[margin:].reshape(TOKENS, KVG * HD).astype(jnp.bfloat16)
    return query_grad, key_grad, value_grad
```

```python
import functools
import math

import jax
import jax.numpy as jnp
from jax import lax
from jax.experimental import pallas as pl
from jax.experimental.pallas import tpu as pltpu
from jax.sharding import PartitionSpec as P

HD = 128
ROWS = 256
GROUP_HEADS = 16
HEADS_STEP = 8
HEAD_DEVS = 8
PIECE = ROWS // HEAD_DEVS
ROW_LEN = 4
SCALE = HD ** (-0.5)
LOG2E = math.log2(math.e)
NT = (((1,), (1,)), ((), ()))
F32 = jnp.float32
BF16 = jnp.bfloat16
VMEM_LIMIT = 56 * 2**20


def slot_base(ctx, slot):
    x = ctx % ROW_LEN
    row = ctx // ROW_LEN
    return ((row - jnp.where(slot > x, 1, 0)) * ROW_LEN + slot) * ROWS


def pack_kernel(keys_ref, values_ref, out_ref):
    for h in range(HEAD_DEVS):
        out_ref[h, 0] = keys_ref[:, h * HD : (h + 1) * HD]
        out_ref[h, 1] = values_ref[:, h * HD : (h + 1) * HD]


def unpack_kernel(pair_ref, keys_ref, values_ref):
    for h in range(HEAD_DEVS):
        keys_ref[:, h * HD : (h + 1) * HD] = pair_ref[h, 0]
        values_ref[:, h * HD : (h + 1) * HD] = pair_ref[h, 1]


def attend(ctx, blocks, mask_ref, kt_ref, kv_ref, acc_ref, q_ref, do_ref, ln_ref, dl_ref, ds_ref, emit):
    n = len(blocks)

    @pl.when(pl.program_id(0) == 0)
    def _():
        acc_ref[...] = jnp.zeros_like(acc_ref)
        q_pos = ctx * ROWS + lax.broadcasted_iota(jnp.int32, (1, ROWS), 1)
        for i, (key, value, base) in enumerate(blocks):
            part = slice(i * ROWS, (i + 1) * ROWS)
            k_pos = base + lax.broadcasted_iota(jnp.int32, (ROWS, ROWS), 0)
            allowed = (k_pos >= ds_ref[...]) & (k_pos <= q_pos)
            mask_ref[part] = jnp.where(allowed, jnp.inf, -jnp.inf)
            key = key().reshape(ROWS, HD)
            kv_ref[0, part] = key
            kv_ref[1, part] = value().reshape(ROWS, HD)
            kt_ref[:, part] = key.T

    for h in range(HEADS_STEP):
        col = slice(h * HD, (h + 1) * HD)
        q = q_ref[:, col]
        do = do_ref[:, col]
        scores = lax.dot_general(kv_ref[0], q, NT, preferred_element_type=F32)
        dprobs = lax.dot_general(kv_ref[1], do, NT, preferred_element_type=F32)
        power = scores * (SCALE * LOG2E) - ln_ref[h : h + 1, :] * LOG2E
        probs = jnp.exp2(jnp.minimum(power, mask_ref[...]))
        dscores = (probs * (dprobs - dl_ref[h : h + 1, :])).astype(BF16)
        acc_ref[1] += jnp.dot(probs.astype(BF16), do, preferred_element_type=F32)
        acc_ref[0] += jnp.dot(dscores, q, preferred_element_type=F32)
        emit(col, jnp.dot(kt_ref[...], dscores, preferred_element_type=F32).T)


def near_kernel(ctx_ref, own_ref, prev_ref, q_ref, do_ref, ln_ref, dl_ref, ds_ref,
                dq_ref, grads_ref, acc_ref, mask_ref, kv_ref, kt_ref):
    ctx = ctx_ref[0]
    blocks = [
        (lambda: own_ref[:, 0], lambda: own_ref[:, 1], ctx * ROWS),
        (lambda: prev_ref[:, 0], lambda: prev_ref[:, 1], (ctx - ROW_LEN) * ROWS),
    ]

    def emit(col, value):
        dq_ref[:, col] = value

    attend(ctx, blocks, mask_ref, kt_ref, kv_ref, acc_ref, q_ref, do_ref, ln_ref, dl_ref, ds_ref, emit)

    @pl.when(pl.program_id(0) == pl.num_programs(0) - 1)
    def _():
        for i in range(2):
            part = slice(i * ROWS, (i + 1) * ROWS)
            grads_ref[i, :, 0] = (acc_ref[0, part] * SCALE).reshape(HEAD_DEVS, PIECE, HD)
            grads_ref[i, :, 1] = acc_ref[1, part].reshape(HEAD_DEVS, PIECE, HD)


def rest_kernel(ctx_ref, slots_ref, q_ref, do_ref, ln_ref, dl_ref, ds_ref, dq_near_ref,
                dq_ref, grads_ref, acc_ref, mask_ref, kv_ref, kt_ref):
    ctx = ctx_ref[0]
    x = ctx % ROW_LEN
    slots = [(x + 1 + i) % ROW_LEN for i in range(ROW_LEN - 1)]
    blocks = [
        (lambda s=s: slots_ref[s, :, 0], lambda s=s: slots_ref[s, :, 1], slot_base(ctx, s))
        for s in slots
    ]

    def emit(col, value):
        dq_ref[:, col] = ((value + dq_near_ref[:, col]) * SCALE).astype(BF16)

    attend(ctx, blocks, mask_ref, kt_ref, kv_ref, acc_ref, q_ref, do_ref, ln_ref, dl_ref, ds_ref, emit)

    @pl.when(pl.program_id(0) == pl.num_programs(0) - 1)
    def _():
        grads_ref[x] = jnp.zeros((HEAD_DEVS, 2, PIECE, HD), BF16)
        for i, s in enumerate(slots):
            part = slice(i * ROWS, (i + 1) * ROWS)
            grads_ref[s, :, 0] = (acc_ref[0, part] * SCALE).astype(BF16).reshape(HEAD_DEVS, PIECE, HD)
            grads_ref[s, :, 1] = acc_ref[1, part].astype(BF16).reshape(HEAD_DEVS, PIECE, HD)


def attention_call(kernel, count, extra_in, dq_type, grads, name):
    def whole(shape):
        return pl.BlockSpec(shape, lambda g: (0,) * len(shape))

    wide = pl.BlockSpec((ROWS, HEADS_STEP * HD), lambda g: (0, g))
    stat = pl.BlockSpec((HEADS_STEP, ROWS), lambda g: (g, 0))
    block = (HEAD_DEVS, 2, PIECE, HD)
    block_specs = [whole(block)] * 2 if count == 2 else [whole((ROW_LEN, *block))]
    return pl.pallas_call(
        kernel,
        grid=(GROUP_HEADS // HEADS_STEP,),
        out_shape=(jax.ShapeDtypeStruct((ROWS, GROUP_HEADS * HD), dq_type), grads),
        in_specs=[pl.BlockSpec(memory_space=pltpu.SMEM), *block_specs, wide, wide, stat, stat,
                  whole((1, ROWS))] + [wide] * extra_in,
        out_specs=(wide, whole(grads.shape)),
        scratch_shapes=[
            pltpu.VMEM((2, count * ROWS, HD), F32),
            pltpu.VMEM((count * ROWS, ROWS), F32),
            pltpu.VMEM((2, count * ROWS, HD), BF16),
            pltpu.VMEM((HD, count * ROWS), BF16),
        ],
        compiler_params=pltpu.CompilerParams(vmem_limit_bytes=VMEM_LIMIT),
        name=name,
    )


def gather_kernel(ctx_ref, back_ref, near_ref, own_ref, prev_ref):
    x = ctx_ref[0] % ROW_LEN
    own = near_ref[0]
    prev = near_ref[1]
    for s in range(ROW_LEN):
        term = back_ref[s].astype(F32)
        own = own + jnp.where(s > x, term, 0.0)
        prev = prev + jnp.where(s < x, term, 0.0)
    own_ref[...] = own
    prev_ref[...] = prev.astype(BF16)


def local(width, queries, keys, values, out_grad, log_norm, delta_rows, doc_start):
    ctx = lax.axis_index("ctx").astype(jnp.int32)
    x = ctx % ROW_LEN
    ctx_arr = ctx.reshape(1)
    first = doc_start.reshape(1, ROWS)
    block = (HEAD_DEVS, 2, PIECE, HD)
    rows = [[r * ROW_LEN + s for s in range(ROW_LEN)] for r in range(width // ROW_LEN)]
    up = [(i, i + ROW_LEN) for i in range(width - ROW_LEN)]
    down = [(i + ROW_LEN, i) for i in range(width - ROW_LEN)]

    packed = pl.pallas_call(pack_kernel, out_shape=jax.ShapeDtypeStruct(block, BF16), name="pack")(keys, values)
    own = lax.all_to_all(packed, "head", split_axis=0, concat_axis=0, tiled=True)
    prev = lax.ppermute(own, "ctx", up)
    slot = lax.broadcasted_iota(jnp.int32, (ROW_LEN, 1, 1, 1, 1), 0)
    outgoing = jnp.where(slot > x, own[None], prev[None])
    slots = lax.all_to_all(outgoing, "ctx", split_axis=0, concat_axis=0, tiled=True, axis_index_groups=rows)

    dq_near, near = attention_call(
        near_kernel, 2, 0, F32, jax.ShapeDtypeStruct((2, *block), F32), "near"
    )(ctx_arr, own, prev, queries, out_grad, log_norm, delta_rows, first)
    query_grad, rest = attention_call(
        rest_kernel, 3, 1, BF16, jax.ShapeDtypeStruct((ROW_LEN, *block), BF16), "rest"
    )(ctx_arr, slots, queries, out_grad, log_norm, delta_rows, first, dq_near)

    back = lax.all_to_all(rest, "ctx", split_axis=0, concat_axis=0, tiled=True, axis_index_groups=rows)
    own_sum, prev_sum = pl.pallas_call(
        gather_kernel,
        in_specs=[pl.BlockSpec(memory_space=pltpu.SMEM)] + [pl.BlockSpec(memory_space=pltpu.VMEM)] * 2,
        out_shape=(jax.ShapeDtypeStruct(block, F32), jax.ShapeDtypeStruct(block, BF16)),
        name="gather",
    )(ctx_arr, back, near)
    from_next = lax.ppermute(prev_sum, "ctx", down)
    total = (own_sum + from_next.astype(F32)).astype(BF16)
    returned = lax.all_to_all(total, "head", split_axis=0, concat_axis=0, tiled=True)
    key_grad, value_grad = pl.pallas_call(
        unpack_kernel,
        out_shape=(jax.ShapeDtypeStruct((PIECE, HEAD_DEVS * HD), BF16),) * 2,
        name="unpack",
    )(returned)
    return query_grad, key_grad, value_grad


def solution(mesh):
    return jax.shard_map(
        functools.partial(local, mesh.shape["ctx"]),
        mesh=mesh,
        in_specs=(
            P("ctx", "head"),
            P(("ctx", "head"), None),
            P(("ctx", "head"), None),
            P("ctx", "head"),
            P("head", "ctx"),
            P("head", "ctx"),
            P("ctx"),
        ),
        out_specs=(P("ctx", "head"), P(("ctx", "head"), None), P(("ctx", "head"), None)),
        check_vma=False,
    )
```

```python
import functools
import math

import jax
import jax.numpy as jnp
from jax import lax
from jax.experimental import pallas as pl
from jax.experimental.pallas import tpu as pltpu
from jax.sharding import PartitionSpec as P

HD = 128
ROWS = 256
GROUP_HEADS = 16
HEAD_DEVS = 8
PIECE = ROWS // HEAD_DEVS
ROW_LEN = 4
SCALE = HD ** (-0.5)
LOG2E = math.log2(math.e)
NT = (((1,), (1,)), ((), ()))
F32 = jnp.float32
BF16 = jnp.bfloat16
VMEM_LIMIT = 14 * 2**20


def slot_base(ctx, slot):
    x = ctx % ROW_LEN
    row = ctx // ROW_LEN
    return ((row - jnp.where(slot > x, 1, 0)) * ROW_LEN + slot) * ROWS


def pack_kernel(keys_ref, values_ref, out_ref):
    for h in range(HEAD_DEVS):
        out_ref[h, 0] = keys_ref[:, h * HD : (h + 1) * HD]
        out_ref[h, 1] = values_ref[:, h * HD : (h + 1) * HD]


def unpack_kernel(pair_ref, keys_ref, values_ref):
    for h in range(HEAD_DEVS):
        keys_ref[:, h * HD : (h + 1) * HD] = pair_ref[h, 0]
        values_ref[:, h * HD : (h + 1) * HD] = pair_ref[h, 1]


def attend(ctx, blocks, mask_ref, kt_ref, kv_ref, acc_ref, q_ref, do_ref, ln_ref, dl_ref, ds_ref, emit):
    q_pos = ctx * ROWS + lax.broadcasted_iota(jnp.int32, (1, ROWS), 1)
    for i, (ref, base) in enumerate(blocks):
        part = slice(i * ROWS, (i + 1) * ROWS)
        k_pos = base + lax.broadcasted_iota(jnp.int32, (ROWS, ROWS), 0)
        allowed = (k_pos >= ds_ref[...]) & (k_pos <= q_pos)
        mask_ref[part] = jnp.where(allowed, jnp.inf, -jnp.inf)
        key = ref[:, 0].reshape(ROWS, HD)
        kv_ref[0, part] = key
        kv_ref[1, part] = ref[:, 1].reshape(ROWS, HD)
        kt_ref[:, part] = key.T

    for h in range(GROUP_HEADS):
        col = slice(h * HD, (h + 1) * HD)
        q = q_ref[:, col]
        do = do_ref[:, col]
        scores = lax.dot_general(kv_ref[0], q, NT, preferred_element_type=F32)
        dprobs = lax.dot_general(kv_ref[1], do, NT, preferred_element_type=F32)
        power = scores * (SCALE * LOG2E) - ln_ref[h : h + 1, :] * LOG2E
        probs = jnp.exp2(jnp.minimum(power, mask_ref[...]))
        dscores = (probs * (dprobs - dl_ref[h : h + 1, :])).astype(BF16)
        value_term = jnp.dot(probs.astype(BF16), do, preferred_element_type=F32)
        key_term = jnp.dot(dscores, q, preferred_element_type=F32)
        if h:
            value_term += acc_ref[1]
            key_term += acc_ref[0]
        acc_ref[1] = value_term
        acc_ref[0] = key_term
        emit(col, jnp.dot(kt_ref[...], dscores, preferred_element_type=F32).T)


def put_grads(ref, acc_ref, part):
    ref[:, 0] = (acc_ref[0, part] * SCALE).astype(ref.dtype).reshape(HEAD_DEVS, PIECE, HD)
    ref[:, 1] = acc_ref[1, part].astype(ref.dtype).reshape(HEAD_DEVS, PIECE, HD)


def one_kernel(offset, ctx_ref, block_ref, q_ref, do_ref, ln_ref, dl_ref, ds_ref,
               dq_ref, grads_ref, acc_ref, mask_ref, kv_ref, kt_ref):
    ctx = ctx_ref[0]

    def emit(col, value):
        dq_ref[:, col] = value.astype(BF16)

    attend(ctx, [(block_ref, (ctx - offset) * ROWS)], mask_ref, kt_ref, kv_ref, acc_ref, q_ref, do_ref, ln_ref, dl_ref, ds_ref, emit)
    put_grads(grads_ref, acc_ref, slice(None))


def rest_kernel(ctx_ref, slots_ref, q_ref, do_ref, ln_ref, dl_ref, ds_ref,
                dq_ref, grads_ref, acc_ref, mask_ref, kv_ref, kt_ref):
    ctx = ctx_ref[0]
    x = ctx % ROW_LEN
    slots = [(x + 1 + i) % ROW_LEN for i in range(ROW_LEN - 1)]

    def emit(col, value):
        dq_ref[:, col] = value.astype(BF16)

    blocks = [(slots_ref.at[s], slot_base(ctx, s)) for s in slots]
    attend(ctx, blocks, mask_ref, kt_ref, kv_ref, acc_ref, q_ref, do_ref, ln_ref, dl_ref, ds_ref, emit)
    grads_ref[x] = jnp.zeros((HEAD_DEVS, 2, PIECE, HD), BF16)
    for i, s in enumerate(slots):
        put_grads(grads_ref.at[s], acc_ref, slice(i * ROWS, (i + 1) * ROWS))


def vmem_call(kernel, out, *args, name, scratch=()):
    specs = [pl.BlockSpec(memory_space=pltpu.SMEM if a.size == 1 else pltpu.VMEM) for a in args]
    outs = jax.tree.map(lambda _: pl.BlockSpec(memory_space=pltpu.VMEM), out)
    return pl.pallas_call(
        kernel,
        out_shape=out,
        in_specs=specs,
        out_specs=outs,
        scratch_shapes=scratch,
        compiler_params=pltpu.CompilerParams(vmem_limit_bytes=VMEM_LIMIT),
        name=name,
    )(*args)


def attention_call(kernel, count, grads, name, *args):
    scratch = [
        pltpu.VMEM((2, count * ROWS, HD), F32),
        pltpu.VMEM((count * ROWS, ROWS), F32),
        pltpu.VMEM((2, count * ROWS, HD), BF16),
        pltpu.VMEM((HD, count * ROWS), BF16),
    ]
    dq = jax.ShapeDtypeStruct((ROWS, GROUP_HEADS * HD), BF16)
    return vmem_call(kernel, (dq, grads), *args, name=name, scratch=scratch)


def prev_sum_kernel(ctx_ref, back_ref, near_ref, out_ref):
    x = ctx_ref[0] % ROW_LEN
    total = near_ref[...]
    for s in range(ROW_LEN):
        total = total + jnp.where(s < x, back_ref[s].astype(F32), 0.0)
    out_ref[...] = total.astype(BF16)


def own_sum_kernel(ctx_ref, back_ref, near_ref, out_ref):
    x = ctx_ref[0] % ROW_LEN
    total = near_ref[...]
    for s in range(ROW_LEN):
        total = total + jnp.where(s > x, back_ref[s].astype(F32), 0.0)
    out_ref[...] = total


def add_kernel(a_ref, b_ref, out_ref):
    out_ref[...] = (a_ref[...] + b_ref[...].astype(F32)).astype(BF16)


def local(width, queries, keys, values, out_grad, log_norm, delta_rows, doc_start):
    ctx = lax.axis_index("ctx").astype(jnp.int32)
    x = ctx % ROW_LEN
    ctx_arr = ctx.reshape(1)
    first = doc_start.reshape(1, ROWS)
    block = (HEAD_DEVS, 2, PIECE, HD)
    rows = [[r * ROW_LEN + s for s in range(ROW_LEN)] for r in range(width // ROW_LEN)]
    up = [(i, i + ROW_LEN) for i in range(width - ROW_LEN)]
    down = [(i + ROW_LEN, i) for i in range(width - ROW_LEN)]

    pieces = jax.ShapeDtypeStruct(block, BF16)
    pieces_f32 = jax.ShapeDtypeStruct(block, F32)
    slots_type = jax.ShapeDtypeStruct((ROW_LEN, *block), BF16)
    side = (queries, out_grad, log_norm, delta_rows, first)

    packed = pl.pallas_call(pack_kernel, out_shape=pieces, name="pack")(keys, values)
    own = lax.all_to_all(packed, "head", split_axis=0, concat_axis=0, tiled=True)
    prev = lax.ppermute(own, "ctx", up)
    slot = lax.broadcasted_iota(jnp.int32, (ROW_LEN, 1, 1, 1, 1), 0)
    outgoing = jnp.where(slot > x, own[None], prev[None])
    slots = lax.all_to_all(outgoing, "ctx", split_axis=0, concat_axis=0, tiled=True, axis_index_groups=rows)
    dq_own, own_grads = attention_call(
        functools.partial(one_kernel, 0), 1, pieces_f32, "own", ctx_arr, own, *side
    )
    slots, dq_own = lax.optimization_barrier((slots, dq_own))
    dq_rest, rest = attention_call(rest_kernel, 3, slots_type, "rest", ctx_arr, slots, *side)

    rest, prev = lax.optimization_barrier((rest, prev))
    back = lax.all_to_all(rest, "ctx", split_axis=0, concat_axis=0, tiled=True, axis_index_groups=rows)
    dq_prev, prev_grads = attention_call(
        functools.partial(one_kernel, ROW_LEN), 1, pieces_f32, "prev", ctx_arr, prev, *side
    )
    query_grad = (dq_own.astype(F32) + dq_rest.astype(F32) + dq_prev.astype(F32)) * SCALE
    query_grad = query_grad.astype(BF16)
    prev_sum = vmem_call(prev_sum_kernel, pieces, ctx_arr, back, prev_grads, name="prev_sum")
    from_next = lax.ppermute(prev_sum, "ctx", down)
    own_sum = vmem_call(own_sum_kernel, pieces_f32, ctx_arr, back, own_grads, name="own_sum")
    total = vmem_call(add_kernel, pieces, own_sum, from_next, name="add")
    returned = lax.all_to_all(total, "head", split_axis=0, concat_axis=0, tiled=True)
    tokens = jax.ShapeDtypeStruct((PIECE, HEAD_DEVS * HD), BF16)
    key_grad, value_grad = vmem_call(unpack_kernel, (tokens, tokens), returned, name="unpack")
    return query_grad, key_grad, value_grad


def solution(mesh):
    return jax.shard_map(
        functools.partial(local, mesh.shape["ctx"]),
        mesh=mesh,
        in_specs=(
            P("ctx", "head"),
            P(("ctx", "head"), None),
            P(("ctx", "head"), None),
            P("ctx", "head"),
            P("head", "ctx"),
            P("head", "ctx"),
            P("ctx"),
        ),
        out_specs=(P("ctx", "head"), P(("ctx", "head"), None), P(("ctx", "head"), None)),
        check_vma=False,
    )
```

```python
import functools
import math

import jax
import jax.numpy as jnp
from jax import lax
from jax.experimental import pallas as pl
from jax.experimental.pallas import tpu as pltpu
from jax.sharding import PartitionSpec as P

HD = 128
ROWS = 256
GROUP_HEADS = 16
HEAD_DEVS = 8
PIECE = ROWS // HEAD_DEVS
PART = 4
PARTS = GROUP_HEADS // PART
ROW_LEN = 4
SCALE = HD ** (-0.5)
LOG2E = math.log2(math.e)
NT = (((1,), (1,)), ((), ()))
F32 = jnp.float32
BF16 = jnp.bfloat16
VMEM_LIMIT = 14 * 2**20


def slot_base(ctx, slot):
    x = ctx % ROW_LEN
    row = ctx // ROW_LEN
    return ((row - jnp.where(slot > x, 1, 0)) * ROW_LEN + slot) * ROWS


def pack_kernel(keys_ref, values_ref, starts_ref, out_ref, first_ref, sem, first_sem):
    copies = [
        pltpu.make_async_copy(ref.at[:, pl.ds(h * HD, HD)], out_ref.at[h, i], sem.at[i, h])
        for i, ref in enumerate((keys_ref, values_ref))
        for h in range(HEAD_DEVS)
    ] + [pltpu.make_async_copy(starts_ref, first_ref, first_sem)]
    for copy in copies:
        copy.start()
    for copy in copies:
        copy.wait()


def unpack_kernel(pair_ref, keys_ref, values_ref):
    for h in range(HEAD_DEVS):
        keys_ref[:, h * HD : (h + 1) * HD] = pair_ref[h, 0]
        values_ref[:, h * HD : (h + 1) * HD] = pair_ref[h, 1]


def attend(ctx, blocks, mask_ref, kt_ref, kv_ref, acc_ref, q_ref, do_ref, ln_ref, dl_ref, ds_ref, emit):
    q_pos = ctx * ROWS + lax.broadcasted_iota(jnp.int32, (1, ROWS), 1)
    for i, (ref, base) in enumerate(blocks):
        part = slice(i * ROWS, (i + 1) * ROWS)
        k_pos = base + lax.broadcasted_iota(jnp.int32, (ROWS, ROWS), 0)
        allowed = (k_pos >= ds_ref[...]) & (k_pos <= q_pos)
        mask_ref[part] = jnp.where(allowed, jnp.inf, -jnp.inf)
        key = ref[:, 0].reshape(ROWS, HD)
        kv_ref[0, part] = key
        kv_ref[1, part] = ref[:, 1].reshape(ROWS, HD)
        kt_ref[:, part] = key.T

    for h in range(GROUP_HEADS):
        col = slice(h * HD, (h + 1) * HD)
        q = q_ref[:, col]
        do = do_ref[:, col]
        scores = lax.dot_general(kv_ref[0], q, NT, preferred_element_type=F32)
        dprobs = lax.dot_general(kv_ref[1], do, NT, preferred_element_type=F32)
        power = scores * (SCALE * LOG2E) - ln_ref[h : h + 1, :] * LOG2E
        probs = jnp.exp2(jnp.minimum(power, mask_ref[...]))
        dscores = (probs * (dprobs - dl_ref[h : h + 1, :])).astype(BF16)
        value_term = jnp.dot(probs.astype(BF16), do, preferred_element_type=F32)
        key_term = jnp.dot(dscores, q, preferred_element_type=F32)
        if h:
            value_term += acc_ref[1]
            key_term += acc_ref[0]
        acc_ref[1] = value_term
        acc_ref[0] = key_term
        emit(col, jnp.dot(kt_ref[...], dscores, preferred_element_type=F32).T)


def put_grads(ref, acc_ref, part):
    ref[:, 0] = (acc_ref[0, part] * SCALE).astype(ref.dtype).reshape(HEAD_DEVS, PIECE, HD)
    ref[:, 1] = acc_ref[1, part].astype(ref.dtype).reshape(HEAD_DEVS, PIECE, HD)


def part_copies(src, dst, sem):
    cols = [pl.ds(p * PART * HD, PART * HD) for p in range(PARTS)]
    return [pltpu.make_async_copy(src.at[:, c], dst.at[:, c], sem.at[p]) for p, c in enumerate(cols)]


class Sender:
    def __init__(self, dq_ref, buf, sem):
        self.buf = buf
        self.copies = part_copies(buf, dq_ref, sem)

    def __call__(self, col, value):
        part, head = divmod(col.start // HD, PART)
        self.buf[:, col] = value.astype(BF16)
        if head == PART - 1:
            self.copies[part].start()

    def finish(self):
        for copy in self.copies:
            copy.wait()


def own_kernel(ctx_ref, own_ref, q_ref, do_ref, ln_ref, dl_ref, ds_ref,
               dq_ref, grads_ref, acc_ref, mask_ref, kv_ref, kt_ref, buf, sem):
    ctx = ctx_ref[0]
    emit = Sender(dq_ref, buf, sem)
    attend(ctx, [(own_ref, ctx * ROWS)], mask_ref, kt_ref, kv_ref, acc_ref, q_ref, do_ref, ln_ref, dl_ref, ds_ref, emit)
    put_grads(grads_ref, acc_ref, slice(None))
    emit.finish()


def prev_kernel(ctx_ref, prev_ref, q_ref, do_ref, ln_ref, dl_ref, ds_ref, dq_own_ref, dq_rest_ref,
                dq_ref, grads_ref, acc_ref, mask_ref, kv_ref, kt_ref, buf, sem, total, own_buf, rest_buf, part_sem):
    ctx = ctx_ref[0]
    fetches = part_copies(dq_own_ref, own_buf, part_sem.at[0])
    fetches += part_copies(dq_rest_ref, rest_buf, part_sem.at[1])
    copies = part_copies(buf, dq_ref, sem)
    for fetch in fetches:
        fetch.start()

    def emit(col, value):
        total[:, col] = value
        part, head = divmod(col.start // HD, PART)
        if head < PART - 1 or part < PARTS // 2:
            return
        if part == PARTS // 2:
            for fetch in fetches:
                fetch.wait()
        for p in range(part + 1) if part == PARTS // 2 else [part]:
            cols = slice(p * PART * HD, (p + 1) * PART * HD)
            value = total[:, cols] + own_buf[:, cols].astype(F32) + rest_buf[:, cols].astype(F32)
            buf[:, cols] = (value * SCALE).astype(BF16)
            copies[p].start()

    blocks = [(prev_ref, (ctx - ROW_LEN) * ROWS)]
    attend(ctx, blocks, mask_ref, kt_ref, kv_ref, acc_ref, q_ref, do_ref, ln_ref, dl_ref, ds_ref, emit)
    put_grads(grads_ref, acc_ref, slice(None))
    for copy in copies:
        copy.wait()


def rest_kernel(ctx_ref, slots_ref, q_ref, do_ref, ln_ref, dl_ref, ds_ref,
                dq_ref, grads_ref, acc_ref, mask_ref, kv_ref, kt_ref, buf, sem):
    ctx = ctx_ref[0]
    x = ctx % ROW_LEN
    slots = [(x + 1 + i) % ROW_LEN for i in range(ROW_LEN - 1)]
    blocks = [(slots_ref.at[s], slot_base(ctx, s)) for s in slots]
    emit = Sender(dq_ref, buf, sem)
    attend(ctx, blocks, mask_ref, kt_ref, kv_ref, acc_ref, q_ref, do_ref, ln_ref, dl_ref, ds_ref, emit)
    grads_ref[x] = jnp.zeros((HEAD_DEVS, 2, PIECE, HD), BF16)
    for i, s in enumerate(slots):
        put_grads(grads_ref.at[s], acc_ref, slice(i * ROWS, (i + 1) * ROWS))
    emit.finish()


def vmem_call(kernel, out, *args, name, scratch=(), far=(), far_out=()):
    def space(i, size):
        return pltpu.HBM if i in far else pltpu.SMEM if size == 1 else pltpu.VMEM

    specs = [pl.BlockSpec(memory_space=space(i, a.size)) for i, a in enumerate(args)]
    outs = tuple(pl.BlockSpec(memory_space=pltpu.HBM if i in far_out else pltpu.VMEM) for i in range(len(out)))
    args = [pltpu.with_memory_space_constraint(a, pltpu.HBM) if i in far else a for i, a in enumerate(args)]
    out = tuple(pltpu.HBM(o.shape, o.dtype) if i in far_out else o for i, o in enumerate(out))
    return pl.pallas_call(
        kernel,
        out_shape=out,
        in_specs=specs,
        out_specs=outs,
        scratch_shapes=scratch,
        compiler_params=pltpu.CompilerParams(vmem_limit_bytes=VMEM_LIMIT),
        name=name,
    )(*args)


def attention_call(kernel, count, outs, name, *args, far=(), scratch=()):
    wide = (ROWS, GROUP_HEADS * HD)
    scratch = [
        pltpu.VMEM((2, count * ROWS, HD), F32),
        pltpu.VMEM((count * ROWS, ROWS), F32),
        pltpu.VMEM((2, count * ROWS, HD), BF16),
        pltpu.VMEM((HD, count * ROWS), BF16),
        pltpu.VMEM(wide, BF16),
        pltpu.SemaphoreType.DMA((PARTS,)),
        *scratch,
    ]
    far_at = range(len(args), len(args) + len(far))
    outs = (jax.ShapeDtypeStruct(wide, BF16), *outs)
    return vmem_call(kernel, outs, *args, *far, name=name, scratch=scratch, far=far_at, far_out=(0,))


def prev_sum_kernel(ctx_ref, back_ref, near_ref, out_ref):
    x = ctx_ref[0] % ROW_LEN
    total = near_ref[...]
    for s in range(ROW_LEN):
        total = total + jnp.where(s < x, back_ref[s].astype(F32), 0.0)
    out_ref[...] = total.astype(BF16)


def own_sum_kernel(ctx_ref, back_ref, near_ref, out_ref):
    x = ctx_ref[0] % ROW_LEN
    total = near_ref[...]
    for s in range(ROW_LEN):
        total = total + jnp.where(s > x, back_ref[s].astype(F32), 0.0)
    out_ref[...] = total


def add_kernel(a_ref, b_ref, out_ref):
    out_ref[...] = (a_ref[...] + b_ref[...].astype(F32)).astype(BF16)


def local(width, queries, keys, values, out_grad, log_norm, delta_rows, doc_start):
    ctx = lax.axis_index("ctx").astype(jnp.int32)
    x = ctx % ROW_LEN
    ctx_arr = ctx.reshape(1)
    block = (HEAD_DEVS, 2, PIECE, HD)
    rows = [[r * ROW_LEN + s for s in range(ROW_LEN)] for r in range(width // ROW_LEN)]
    up = [(i, i + ROW_LEN) for i in range(width - ROW_LEN)]
    down = [(i + ROW_LEN, i) for i in range(width - ROW_LEN)]

    pieces = jax.ShapeDtypeStruct(block, BF16)
    pieces_f32 = jax.ShapeDtypeStruct(block, F32)
    slots_type = jax.ShapeDtypeStruct((ROW_LEN, *block), BF16)
    packed, first = vmem_call(
        pack_kernel,
        (pieces, jax.ShapeDtypeStruct((1, ROWS), jnp.int32)),
        keys,
        values,
        doc_start.reshape(1, ROWS),
        name="pack",
        scratch=(pltpu.SemaphoreType.DMA((2, HEAD_DEVS)), pltpu.SemaphoreType.DMA(())),
        far=(0, 1, 2),
    )
    side = (queries, out_grad, log_norm, delta_rows, first)
    own = lax.all_to_all(packed, "head", split_axis=0, concat_axis=0, tiled=True)
    prev = lax.ppermute(own, "ctx", up)
    slot = lax.broadcasted_iota(jnp.int32, (ROW_LEN, 1, 1, 1, 1), 0)
    outgoing = jnp.where(slot > x, own[None], prev[None])
    slots = lax.all_to_all(outgoing, "ctx", split_axis=0, concat_axis=0, tiled=True, axis_index_groups=rows)
    dq_own, own_grads = attention_call(own_kernel, 1, (pieces_f32,), "own", ctx_arr, own, *side)
    slots, dq_own = lax.optimization_barrier((slots, dq_own))
    dq_rest, rest = attention_call(rest_kernel, 3, (slots_type,), "rest", ctx_arr, slots, *side)

    rest, prev = lax.optimization_barrier((rest, prev))
    back = lax.all_to_all(rest, "ctx", split_axis=0, concat_axis=0, tiled=True, axis_index_groups=rows)
    wide = (ROWS, GROUP_HEADS * HD)
    query_grad, prev_grads = attention_call(
        prev_kernel, 1, (pieces_f32,), "prev", ctx_arr, prev, *side, far=(dq_own, dq_rest),
        scratch=(
            pltpu.VMEM(wide, F32),
            pltpu.VMEM(wide, BF16),
            pltpu.VMEM(wide, BF16),
            pltpu.SemaphoreType.DMA((2, PARTS)),
        ),
    )
    (prev_sum,) = vmem_call(prev_sum_kernel, (pieces,), ctx_arr, back, prev_grads, name="prev_sum")
    from_next = lax.ppermute(prev_sum, "ctx", down)
    (own_sum,) = vmem_call(own_sum_kernel, (pieces_f32,), ctx_arr, back, own_grads, name="own_sum")
    (total,) = vmem_call(add_kernel, (pieces,), own_sum, from_next, name="add")
    returned = lax.all_to_all(total, "head", split_axis=0, concat_axis=0, tiled=True)
    tokens = jax.ShapeDtypeStruct((PIECE, HEAD_DEVS * HD), BF16)
    key_grad, value_grad = vmem_call(unpack_kernel, (tokens, tokens), returned, name="unpack")
    return query_grad, key_grad, value_grad


def solution(mesh):
    return jax.shard_map(
        functools.partial(local, mesh.shape["ctx"]),
        mesh=mesh,
        in_specs=(
            P("ctx", "head"),
            P(("ctx", "head"), None),
            P(("ctx", "head"), None),
            P("ctx", "head"),
            P("head", "ctx"),
            P("head", "ctx"),
            P("ctx"),
        ),
        out_specs=(P("ctx", "head"), P(("ctx", "head"), None), P(("ctx", "head"), None)),
        check_vma=False,
    )
```

```python
import functools
import math

import jax
import jax.numpy as jnp
from jax import lax
from jax.experimental import pallas as pl
from jax.experimental.pallas import tpu as pltpu
from jax.sharding import PartitionSpec as P

HD = 128
ROWS = 256
GROUP_HEADS = 16
HEAD_DEVS = 8
PIECE = ROWS // HEAD_DEVS
PART = 4
PARTS = GROUP_HEADS // PART
ROW_LEN = 4
SCALE = HD ** (-0.5)
LOG2E = math.log2(math.e)
NT = (((1,), (1,)), ((), ()))
F32 = jnp.float32
BF16 = jnp.bfloat16
VMEM_LIMIT = 14 * 2**20


def slot_base(ctx, slot):
    x = ctx % ROW_LEN
    row = ctx // ROW_LEN
    return ((row - jnp.where(slot > x, 1, 0)) * ROW_LEN + slot) * ROWS


def pack_kernel(keys_ref, values_ref, starts_ref, out_ref, first_ref, sem, first_sem):
    copies = [
        pltpu.make_async_copy(ref.at[:, pl.ds(h * HD, HD)], out_ref.at[h, i], sem.at[i, h])
        for i, ref in enumerate((keys_ref, values_ref))
        for h in range(HEAD_DEVS)
    ] + [pltpu.make_async_copy(starts_ref, first_ref, first_sem)]
    for copy in copies:
        copy.start()
    for copy in copies:
        copy.wait()


def unpack_kernel(pair_ref, keys_ref, values_ref, sem):
    copies = [
        pltpu.make_async_copy(pair_ref.at[h, i], ref.at[:, pl.ds(h * HD, HD)], sem.at[i, h])
        for i, ref in enumerate((keys_ref, values_ref))
        for h in range(HEAD_DEVS)
    ]
    for copy in copies:
        copy.start()
    for copy in copies:
        copy.wait()


def fill_kernel(ctx_ref, own_ref, prev_ref, out_ref, sem):
    x = ctx_ref[0] % ROW_LEN
    for s in range(ROW_LEN):
        for ref, ours in ((own_ref, s > x), (prev_ref, s <= x)):

            @pl.when(ours)
            def _(ref=ref):
                pltpu.make_async_copy(ref, out_ref.at[s], sem.at[s]).start()

    for s in range(ROW_LEN):
        pltpu.make_async_copy(own_ref, out_ref.at[s], sem.at[s]).wait()


def attend(ctx, blocks, mask_ref, kt_ref, kv_ref, acc_ref, q_ref, do_ref, ln_ref, dl_ref, ds_ref, emit):
    q_pos = ctx * ROWS + lax.broadcasted_iota(jnp.int32, (1, ROWS), 1)
    for i, (ref, base) in enumerate(blocks):
        part = slice(i * ROWS, (i + 1) * ROWS)
        k_pos = base + lax.broadcasted_iota(jnp.int32, (ROWS, ROWS), 0)
        allowed = (k_pos >= ds_ref[...]) & (k_pos <= q_pos)
        mask_ref[part] = jnp.where(allowed, jnp.inf, -jnp.inf)
        key = ref[:, 0].reshape(ROWS, HD)
        kv_ref[0, part] = key
        kv_ref[1, part] = ref[:, 1].reshape(ROWS, HD)
        kt_ref[:, part] = key.T

    for h in range(GROUP_HEADS):
        col = slice(h * HD, (h + 1) * HD)
        q = q_ref[:, col]
        do = do_ref[:, col]
        scores = lax.dot_general(kv_ref[0], q, NT, preferred_element_type=F32)
        dprobs = lax.dot_general(kv_ref[1], do, NT, preferred_element_type=F32)
        power = scores * (SCALE * LOG2E) - ln_ref[h : h + 1, :] * LOG2E
        probs = jnp.exp2(jnp.minimum(power, mask_ref[...]))
        dscores = (probs * (dprobs - dl_ref[h : h + 1, :])).astype(BF16)
        value_term = jnp.dot(probs.astype(BF16), do, preferred_element_type=F32)
        key_term = jnp.dot(dscores, q, preferred_element_type=F32)
        if h:
            value_term += acc_ref[1]
            key_term += acc_ref[0]
        acc_ref[1] = value_term
        acc_ref[0] = key_term
        emit(col, jnp.dot(kt_ref[...], dscores, preferred_element_type=F32).T)


def put_grads(ref, acc_ref, part):
    ref[:, 0] = (acc_ref[0, part] * SCALE).astype(ref.dtype).reshape(HEAD_DEVS, PIECE, HD)
    ref[:, 1] = acc_ref[1, part].astype(ref.dtype).reshape(HEAD_DEVS, PIECE, HD)


def part_copies(src, dst, sem):
    cols = [pl.ds(p * PART * HD, PART * HD) for p in range(PARTS)]
    return [pltpu.make_async_copy(src.at[:, c], dst.at[:, c], sem.at[p]) for p, c in enumerate(cols)]


class Sender:
    def __init__(self, dq_ref, buf, sem):
        self.buf = buf
        self.copies = part_copies(buf, dq_ref, sem)

    def __call__(self, col, value):
        part, head = divmod(col.start // HD, PART)
        self.buf[:, col] = value.astype(BF16)
        if head == PART - 1:
            self.copies[part].start()

    def finish(self):
        for copy in self.copies:
            copy.wait()


def own_kernel(ctx_ref, own_ref, q_ref, do_ref, ln_ref, dl_ref, ds_ref,
               dq_ref, grads_ref, acc_ref, mask_ref, kv_ref, kt_ref, buf, sem):
    ctx = ctx_ref[0]
    emit = Sender(dq_ref, buf, sem)
    attend(ctx, [(own_ref, ctx * ROWS)], mask_ref, kt_ref, kv_ref, acc_ref, q_ref, do_ref, ln_ref, dl_ref, ds_ref, emit)
    put_grads(grads_ref, acc_ref, slice(None))
    emit.finish()


def prev_kernel(ctx_ref, prev_ref, q_ref, do_ref, ln_ref, dl_ref, ds_ref, dq_own_ref, dq_rest_ref,
                dq_ref, grads_ref, acc_ref, mask_ref, kv_ref, kt_ref, buf, sem, total, own_buf, rest_buf, part_sem):
    ctx = ctx_ref[0]
    fetches = part_copies(dq_own_ref, own_buf, part_sem.at[0])
    fetches += part_copies(dq_rest_ref, rest_buf, part_sem.at[1])
    copies = part_copies(buf, dq_ref, sem)
    for fetch in fetches:
        fetch.start()

    def emit(col, value):
        total[:, col] = value
        part, head = divmod(col.start // HD, PART)
        if head < PART - 1 or part < PARTS // 2:
            return
        if part == PARTS // 2:
            for fetch in fetches:
                fetch.wait()
        for p in range(part + 1) if part == PARTS // 2 else [part]:
            cols = slice(p * PART * HD, (p + 1) * PART * HD)
            value = total[:, cols] + own_buf[:, cols].astype(F32) + rest_buf[:, cols].astype(F32)
            buf[:, cols] = (value * SCALE).astype(BF16)
            copies[p].start()

    blocks = [(prev_ref, (ctx - ROW_LEN) * ROWS)]
    attend(ctx, blocks, mask_ref, kt_ref, kv_ref, acc_ref, q_ref, do_ref, ln_ref, dl_ref, ds_ref, emit)
    put_grads(grads_ref, acc_ref, slice(None))
    for copy in copies:
        copy.wait()


def rest_kernel(ctx_ref, slots_ref, q_ref, do_ref, ln_ref, dl_ref, ds_ref,
                dq_ref, grads_ref, acc_ref, mask_ref, kv_ref, kt_ref, buf, sem):
    ctx = ctx_ref[0]
    x = ctx % ROW_LEN
    slots = [(x + 1 + i) % ROW_LEN for i in range(ROW_LEN - 1)]
    blocks = [(slots_ref.at[s], slot_base(ctx, s)) for s in slots]
    emit = Sender(dq_ref, buf, sem)
    attend(ctx, blocks, mask_ref, kt_ref, kv_ref, acc_ref, q_ref, do_ref, ln_ref, dl_ref, ds_ref, emit)
    grads_ref[x] = jnp.zeros((HEAD_DEVS, 2, PIECE, HD), BF16)
    for i, s in enumerate(slots):
        put_grads(grads_ref.at[s], acc_ref, slice(i * ROWS, (i + 1) * ROWS))
    emit.finish()


def vmem_call(kernel, out, *args, name, scratch=(), far=(), far_out=()):
    def space(i, size):
        return pltpu.HBM if i in far else pltpu.SMEM if size == 1 else pltpu.VMEM

    specs = [pl.BlockSpec(memory_space=space(i, a.size)) for i, a in enumerate(args)]
    outs = tuple(pl.BlockSpec(memory_space=pltpu.HBM if i in far_out else pltpu.VMEM) for i in range(len(out)))
    args = [pltpu.with_memory_space_constraint(a, pltpu.HBM) if i in far else a for i, a in enumerate(args)]
    out = tuple(pltpu.HBM(o.shape, o.dtype) if i in far_out else o for i, o in enumerate(out))
    return pl.pallas_call(
        kernel,
        out_shape=out,
        in_specs=specs,
        out_specs=outs,
        scratch_shapes=scratch,
        compiler_params=pltpu.CompilerParams(vmem_limit_bytes=VMEM_LIMIT),
        name=name,
    )(*args)


def attention_call(kernel, count, outs, name, *args, far=(), scratch=()):
    wide = (ROWS, GROUP_HEADS * HD)
    scratch = [
        pltpu.VMEM((2, count * ROWS, HD), F32),
        pltpu.VMEM((count * ROWS, ROWS), F32),
        pltpu.VMEM((2, count * ROWS, HD), BF16),
        pltpu.VMEM((HD, count * ROWS), BF16),
        pltpu.VMEM(wide, BF16),
        pltpu.SemaphoreType.DMA((PARTS,)),
        *scratch,
    ]
    far_at = range(len(args), len(args) + len(far))
    outs = (jax.ShapeDtypeStruct(wide, BF16), *outs)
    return vmem_call(kernel, outs, *args, *far, name=name, scratch=scratch, far=far_at, far_out=(0,))


def prev_sum_kernel(ctx_ref, back_ref, near_ref, out_ref):
    x = ctx_ref[0] % ROW_LEN
    total = near_ref[...]
    for s in range(ROW_LEN):
        total = total + jnp.where(s < x, back_ref[s].astype(F32), 0.0)
    out_ref[...] = total.astype(BF16)


def own_sum_kernel(ctx_ref, back_ref, near_ref, out_ref):
    x = ctx_ref[0] % ROW_LEN
    total = near_ref[...]
    for s in range(ROW_LEN):
        total = total + jnp.where(s > x, back_ref[s].astype(F32), 0.0)
    out_ref[...] = total


def add_kernel(a_ref, b_ref, out_ref):
    out_ref[...] = (a_ref[...] + b_ref[...].astype(F32)).astype(BF16)


def local(width, queries, keys, values, out_grad, log_norm, delta_rows, doc_start):
    ctx = lax.axis_index("ctx").astype(jnp.int32)
    ctx_arr = ctx.reshape(1)
    block = (HEAD_DEVS, 2, PIECE, HD)
    rows = [[r * ROW_LEN + s for s in range(ROW_LEN)] for r in range(width // ROW_LEN)]
    up = [(i, i + ROW_LEN) for i in range(width - ROW_LEN)]
    down = [(i + ROW_LEN, i) for i in range(width - ROW_LEN)]

    pieces = jax.ShapeDtypeStruct(block, BF16)
    pieces_f32 = jax.ShapeDtypeStruct(block, F32)
    slots_type = jax.ShapeDtypeStruct((ROW_LEN, *block), BF16)
    packed, first = vmem_call(
        pack_kernel,
        (pieces, jax.ShapeDtypeStruct((1, ROWS), jnp.int32)),
        keys,
        values,
        doc_start.reshape(1, ROWS),
        name="pack",
        scratch=(pltpu.SemaphoreType.DMA((2, HEAD_DEVS)), pltpu.SemaphoreType.DMA(())),
        far=(0, 1, 2),
    )
    side = (queries, out_grad, log_norm, delta_rows, first)
    own = lax.all_to_all(packed, "head", split_axis=0, concat_axis=0, tiled=True)
    prev = lax.ppermute(own, "ctx", up)
    (outgoing,) = vmem_call(
        fill_kernel, (slots_type,), ctx_arr, own, prev, name="fill",
        scratch=(pltpu.SemaphoreType.DMA((ROW_LEN,)),), far_out=(0,),
    )
    slots = lax.all_to_all(outgoing, "ctx", split_axis=0, concat_axis=0, tiled=True, axis_index_groups=rows)
    dq_own, own_grads = attention_call(own_kernel, 1, (pieces_f32,), "own", ctx_arr, own, *side)
    slots, dq_own = lax.optimization_barrier((slots, dq_own))
    dq_rest, rest = attention_call(rest_kernel, 3, (slots_type,), "rest", ctx_arr, slots, *side)

    rest, prev = lax.optimization_barrier((rest, prev))
    back = lax.all_to_all(rest, "ctx", split_axis=0, concat_axis=0, tiled=True, axis_index_groups=rows)
    wide = (ROWS, GROUP_HEADS * HD)
    query_grad, prev_grads = attention_call(
        prev_kernel, 1, (pieces_f32,), "prev", ctx_arr, prev, *side, far=(dq_own, dq_rest),
        scratch=(
            pltpu.VMEM(wide, F32),
            pltpu.VMEM(wide, BF16),
            pltpu.VMEM(wide, BF16),
            pltpu.SemaphoreType.DMA((2, PARTS)),
        ),
    )
    (prev_sum,) = vmem_call(prev_sum_kernel, (pieces,), ctx_arr, back, prev_grads, name="prev_sum")
    from_next = lax.ppermute(prev_sum, "ctx", down)
    (own_sum,) = vmem_call(own_sum_kernel, (pieces_f32,), ctx_arr, back, own_grads, name="own_sum")
    (total,) = vmem_call(add_kernel, (pieces,), own_sum, from_next, name="add")
    returned = lax.all_to_all(total, "head", split_axis=0, concat_axis=0, tiled=True)
    tokens = jax.ShapeDtypeStruct((PIECE, HEAD_DEVS * HD), BF16)
    key_grad, value_grad = vmem_call(
        unpack_kernel, (tokens, tokens), returned, name="unpack",
        scratch=(pltpu.SemaphoreType.DMA((2, HEAD_DEVS)),), far_out=(0, 1),
    )
    return query_grad, key_grad, value_grad


def solution(mesh):
    return jax.shard_map(
        functools.partial(local, mesh.shape["ctx"]),
        mesh=mesh,
        in_specs=(
            P("ctx", "head"),
            P(("ctx", "head"), None),
            P(("ctx", "head"), None),
            P("ctx", "head"),
            P("head", "ctx"),
            P("head", "ctx"),
            P("ctx"),
        ),
        out_specs=(P("ctx", "head"), P(("ctx", "head"), None), P(("ctx", "head"), None)),
        check_vma=False,
    )
```
